32 devices in a mesh: lat: 4 (over y, x), ord: 8 (over z, core).
Axes of the slice: x: 2, y: 2, z: 4, core: 2. Of those that a mesh axis runs over, the one named last changes fastest.
Arguments:
- field: bfloat16 [32, 64, 256], P(('lat', 'ord')), may hold values from -6 to 6
- tap_mask: int32 [32, 8, 15], P(('lat', 'ord')), may hold values 0 or 1
- tap_weight: float32 [32, 8, 15], P(('lat', 'ord')), may hold values from -1.4 to 1.4
- basis_mix: bfloat16 [8, 256, 256], replicated, may hold values from -0.125 to 0.125
- order_slots: int32 [32], replicated, may hold values from 0 to 31, each once
- degree_gain: float32 [32, 256], replicated, may hold values from 0.3 to 3
- spectral_mix: bfloat16 [2, 256, 256], replicated, may hold values from -0.25 to 0.25
Outputs:
- spectrum: bfloat16 [32, 32, 2, 256], P('lat', 'ord')
The draws below stay inside these ranges and needn't reach their ends.
Inputs may be any that keep to these rules, and one draw needn't show every extreme that they name: `order_slots`: each order 0 to 31 stands in exactly one slot.
All inputs are finite; a program needn't handle non-finite values. No bound on the sum of `tap_mask` on one device may be relied on, other than what follows from the above.
Results may differ from the reference program's by a relative error of at most 0.0095.
Values may be sent and summed in bfloat16 or wider, within the bound.
A program may use at most 64 MiB of HBM per device.

```python
import math
import jax
import jax.numpy as jnp
from jax import lax

C = 256
NB = 8
TAPS = 15
NLAT = 32
NLON = 64
M = 32


def place_ends(array, key, low, top_value):
    place = [jax.random.randint(jax.random.fold_in(key, axis), (), 0, length) for axis, length in enumerate(array.shape)]
    widest = array.shape.index(max(array.shape))
    beside = place[:widest] + [(place[widest] + 1) % array.shape[widest]] + place[widest + 1:]
    return array.at[tuple(place)].set(low).at[tuple(beside)].set(top_value)


def levels(key, dims, cuts, low, largest):
    def one(position, parts):
        heights = jax.random.uniform(jax.random.fold_in(jax.random.fold_in(key, 6), position), (parts,), jnp.float32, low / len(cuts), largest / len(cuts))
        return jnp.repeat(jnp.exp(heights), dims[position] // parts).reshape((-1,) + (1,) * (len(dims) - position - 1))

    loudness = one(*cuts[0])
    for cut in cuts[1:]:
        loudness = loudness * one(*cut)
    return loudness


def scatter_about(rng, dims, spread, limit, cuts=(), held_as=jnp.bfloat16):
    values = jax.random.normal(rng, dims, jnp.float32) * spread
    if len(cuts) > 0:
        values = levels(rng, dims, cuts, -0.22, 0.18) * values
    return jnp.clip(values, min=-limit, max=limit).astype(held_as)


def setup_inputs(seed: int = 0) -> dict:
    key_list = jax.random.split(jax.random.key(seed), 8)
    field = scatter_about(key_list[0], (NLAT, NLON, C), 1.0, 6.0, ((0, 32),))
    tap_mask = place_ends((jax.random.randint(key_list[1], (NLAT, NB, TAPS), 0, 3) < 2).astype(jnp.int32), jax.random.fold_in(key_list[1], 1), 0, 1)
    tap_weight = scatter_about(key_list[2], (NLAT, NB, TAPS), 0.35, 1.4, ((0, 32),), jnp.float32)
    basis_mix = scatter_about(key_list[3], (NB, C, C), (NB * C) ** -0.5, 0.125)
    order_slots = jax.random.permutation(key_list[4], M).astype(jnp.int32)
    degree_gain = jnp.clip(jnp.exp(jax.random.uniform(key_list[5], (NLAT, C), jnp.float32, math.log(0.3), math.log(3.0))), 0.3, 3.0)
    spectral_mix = scatter_about(key_list[6], (2, C, C), (2 * C) ** -0.5, 0.25)
    return {"field": field, "tap_mask": tap_mask, "tap_weight": tap_weight, "basis_mix": basis_mix, "order_slots": order_slots, "degree_gain": degree_gain, "spectral_mix": spectral_mix}


def fourier_table(order_slots, n_lon):
    orders = order_slots.astype(jnp.int32)
    points = jnp.arange(n_lon, dtype=jnp.int32)
    phase_int = orders[:, None] * points[None, :] % n_lon
    angles = phase_int.astype(jnp.float32) * (2.0 * math.pi / n_lon)
    factor = 1.0 / math.sqrt(n_lon)
    stacked = jnp.stack([jnp.cos(angles) * factor, -jnp.sin(angles) * factor], axis=1)
    return stacked.reshape(2 * orders.shape[0], n_lon).astype(jnp.bfloat16)

def latitude_table(orders, wavenumbers, lat_rows, n_lat):
    phase_int = wavenumbers[None, :, None] * (2 * lat_rows[None, None, :] + 1) % (4 * n_lat)
    angles = phase_int.astype(jnp.float32) * (math.pi / (2 * n_lat))
    factor = math.sqrt(2.0 / n_lat)
    is_even = (orders % 2 == 0)[:, None, None]
    return (jnp.where(is_even, jnp.cos(angles), jnp.sin(angles)) * factor).astype(jnp.bfloat16)

def disco(lat_rows, filters, out_rows):
    running = None
    for lat_step in range(3):
        cycle_rows = lat_rows[lat_step:lat_step + out_rows].astype(jnp.float32)
        for lon_step in range(5):
            shifted = jnp.roll(cycle_rows, 2 - lon_step, axis=1)
            tap_vals = filters[:, :, 5 * lat_step + lon_step]
            tap_term = tap_vals[:, None, :, None] * shifted[:, :, None, :]
            running = tap_term if running is None else running + tap_term
    return running.astype(jnp.bfloat16)

def mixing(spectral_mix):
    real_part = spectral_mix[0]
    imag_part = spectral_mix[1]
    top_rows = jnp.concatenate([real_part, imag_part], axis=1)
    bottom_rows = jnp.concatenate([-imag_part, real_part], axis=1)
    return jnp.concatenate([top_rows, bottom_rows], axis=0)

def reference(field, tap_mask, tap_weight, basis_mix, order_slots, degree_gain, spectral_mix):
    n_lat, n_lon, channels = field.shape
    basis_count = basis_mix.shape[0]
    n_orders = order_slots.shape[0]
    filters = tap_mask.astype(jnp.float32) * tap_weight
    padded = jnp.pad(field, ((1, 1), (0, 0), (0, 0)))
    weights = basis_mix.reshape(basis_count * channels, channels)
    dft_table = fourier_table(order_slots, n_lon).astype(jnp.float32)
    row_block = 16

    def one_block(block_index):
        offset = block_index * row_block
        lat_rows = lax.dynamic_slice_in_dim(padded, offset, row_block + 2, 0)
        filter_rows = lax.dynamic_slice_in_dim(filters, offset, row_block, 0)
        tap_sums = disco(lat_rows, filter_rows, row_block)
        grid_rows = jnp.dot(tap_sums.reshape(row_block * n_lon, basis_count * channels), weights, preferred_element_type=jnp.float32).astype(jnp.bfloat16)
        grid_rows = grid_rows.reshape(row_block, n_lon, channels).astype(jnp.float32)
        spectra = jnp.einsum('fj,rjc->rfc', dft_table, grid_rows)
        return spectra.astype(jnp.bfloat16)
    fourier = lax.map(one_block, jnp.arange(n_lat // row_block, dtype=jnp.int32))
    fourier = fourier.reshape(n_lat, n_orders, 2, channels)
    wavenumbers = jnp.arange(n_lat, dtype=jnp.int32)
    mix_matrix = mixing(spectral_mix)

    def one_slot(slot_index):
        order_one = lax.dynamic_slice_in_dim(order_slots, slot_index, 1)
        lat_basis = latitude_table(order_one, wavenumbers, wavenumbers, n_lat)[0]
        column = lax.dynamic_index_in_dim(fourier, slot_index, 1, keepdims=False)
        coefficients = jnp.dot(lat_basis, column.reshape(n_lat, 2 * channels), preferred_element_type=jnp.float32)
        scaled = (coefficients.reshape(n_lat, 2, channels) * degree_gain[:, None, :]).astype(jnp.bfloat16)
        return jnp.dot(scaled.reshape(n_lat, 2 * channels), mix_matrix, preferred_element_type=jnp.float32).astype(jnp.bfloat16)
    result = lax.map(one_slot, jnp.arange(n_orders, dtype=jnp.int32))
    return jnp.transpose(result, (1, 0, 2)).reshape(n_lat, n_orders, 2, channels)
```

```python
import functools
import math

import jax
import jax.numpy as jnp
from jax import lax
from jax.experimental import pallas as pl
from jax.experimental.pallas import tpu as pltpu
from jax.sharding import PartitionSpec as P

MESH = pl.DeviceIdType.MESH
F32 = jnp.float32
BF16 = jnp.bfloat16
PAD = 8
SLAB = 8


def log2(n):
    assert n & (n - 1) == 0
    return n.bit_length() - 1


def cosine(phase_int, period):
    q = phase_int & (period - 1)
    r = jnp.minimum(q, period - q)
    x = (period // 4 - r).astype(F32) * (2.0 * math.pi / period)
    x2 = x * x
    total = jnp.full_like(x, -1.0 / math.factorial(11))
    for power, sign in ((9, 1.0), (7, -1.0), (5, 1.0), (3, -1.0), (1, 1.0)):
        total = total * x2 + sign / math.factorial(power)
    return total * x


def iota(shape, dim):
    return lax.broadcasted_iota(jnp.int32, shape, dim)


def repeat(count, body):
    if count == 1:
        body(0)
    else:
        pl.loop(0, count)(body)


def kernel(
    dims,
    mask_ref, weight_ref, slots_ref, field_hbm, basis_hbm, gain_hbm, spectral_hbm,
    out_ref,
    rows_in, padded, taps, basis, gain, spectral, grid, table, sent, held, lat_mat,
    local_sem, halo_send, halo_recv, ord_send, ord_recv, lat_send, lat_recv,
):
    n_lat_dev, n_ord_dev, n_lat, n_lon, n_orders, channels, basis_count = dims
    lat_id = lax.axis_index("lat")
    ord_id = lax.axis_index("ord")
    row_id = lat_id * n_ord_dev + ord_id
    slots_here = n_orders // n_ord_dev
    waves = n_lat // n_lat_dev
    per_slab = min(SLAB // 2, slots_here)
    width = 2 * per_slab
    groups = slots_here // per_slab
    has_prev = row_id > 0
    has_next = row_id < n_lat - 1
    prev_dev = ((row_id - 1) // n_ord_dev, (row_id - 1) % n_ord_dev)
    next_dev = ((row_id + 1) // n_ord_dev, (row_id + 1) % n_ord_dev)
    far_prev = jnp.logical_and(ord_id == 0, has_prev)
    far_next = jnp.logical_and(ord_id == n_ord_dev - 1, has_next)

    barrier = pltpu.get_barrier_semaphore()

    @pl.when(far_prev)
    def _():
        pl.semaphore_signal(barrier, inc=1, device_id=prev_dev, device_id_type=MESH)

    @pl.when(far_next)
    def _():
        pl.semaphore_signal(barrier, inc=1, device_id=next_dev, device_id_type=MESH)

    for step in range(1, n_ord_dev):
        pl.semaphore_signal(
            barrier, inc=1, device_id=(lat_id, lax.rem(ord_id + step, n_ord_dev)), device_id_type=MESH
        )
    for step in range(1, n_lat_dev):
        pl.semaphore_signal(
            barrier, inc=1, device_id=(lax.rem(lat_id + step, n_lat_dev), ord_id), device_id_type=MESH
        )

    own_copy = pltpu.make_async_copy(field_hbm, rows_in.at[pl.ds(1, 1)], local_sem.at[0])
    basis_copy = pltpu.make_async_copy(basis_hbm, basis, local_sem.at[1])
    gain_copy = pltpu.make_async_copy(
        gain_hbm.at[pl.ds(pl.multiple_of(lat_id * waves, waves), waves)], gain, local_sem.at[2]
    )
    spectral_copy = pltpu.make_async_copy(spectral_hbm, spectral, local_sem.at[3])
    own_copy.start()
    basis_copy.start()
    gain_copy.start()
    spectral_copy.start()

    @pl.when(jnp.logical_not(has_prev))
    def _():
        rows_in[0] = jnp.zeros(rows_in.shape[1:], BF16)

    @pl.when(jnp.logical_not(has_next))
    def _():
        rows_in[2] = jnp.zeros(rows_in.shape[1:], BF16)

    orders = slots_ref[...]

    def pick(slot_of_row):
        found = iota((slot_of_row.shape[0], n_orders), 1) == slot_of_row
        return jnp.sum(jnp.where(found, orders.astype(F32), 0.0), axis=1, keepdims=True).astype(jnp.int32)

    block_rows = table.shape[0]

    def dft_block(start):
        row = iota((block_rows, 1), 0) + start
        order = pick(row >> 1)
        phase = order * iota((block_rows, n_lon), 1) + (n_lon // 4) * (row & 1)
        table[...] = (cosine(phase, n_lon) * (1.0 / math.sqrt(n_lon))).astype(BF16)

    lat_rows = min(n_lat, 256 // width)
    out_rows = waves * width

    def lat_block(group, part):
        row = iota((out_rows, 1), 0)
        col = iota((1, lat_rows * width), 1)
        wave = (row >> log2(width)) + lat_id * waves
        slot = (row & (width - 1)) >> 1
        order = pick(slot + ord_id * slots_here + group * per_slab)
        lat = (col >> log2(width)) + part * lat_rows
        phase = wave * (2 * lat + 1) + jnp.where((order & 1) == 0, 0, 3 * n_lat)
        value = cosine(phase, 4 * n_lat) * math.sqrt(2.0 / n_lat)
        apart = (row & (width - 1)) ^ (col & (width - 1))
        straight = jnp.where(apart == 0, value, 0.0)
        turned = jnp.where(apart == 1, jnp.where((row & 1) == 0, -value, value), 0.0)
        lat_mat[:out_rows] = straight.astype(BF16)
        lat_mat[out_rows:] = turned.astype(BF16)

    single_dft = block_rows == 2 * n_orders
    single_lat = groups == 1 and lat_rows == n_lat
    if single_dft:
        dft_block(0)

    others = (n_ord_dev - 1) + (n_lat_dev - 1)
    pl.semaphore_wait(barrier, others + far_prev.astype(jnp.int32) + far_next.astype(jnp.int32))

    to_next = pltpu.make_async_remote_copy(
        src_ref=field_hbm, dst_ref=rows_in.at[pl.ds(0, 1)], send_sem=halo_send.at[0],
        recv_sem=halo_recv.at[0], device_id=next_dev, device_id_type=MESH,
    )
    to_prev = pltpu.make_async_remote_copy(
        src_ref=field_hbm, dst_ref=rows_in.at[pl.ds(2, 1)], send_sem=halo_send.at[1],
        recv_sem=halo_recv.at[1], device_id=prev_dev, device_id_type=MESH,
    )
    pl.when(has_next)(to_next.start)
    pl.when(has_prev)(to_prev.start)
    if single_lat:
        lat_block(0, 0)

    def spread(which):
        row = rows_in[which].astype(F32)
        padded[which, pl.ds(PAD, n_lon)] = row
        padded[which, pl.ds(0, PAD)] = row[n_lon - PAD:]
        padded[which, pl.ds(PAD + n_lon, PAD)] = row[:PAD]

    own_copy.wait()
    spread(1)
    pl.when(has_prev)(to_next.wait_recv)
    spread(0)
    pl.when(has_next)(to_prev.wait_recv)
    spread(2)

    lon_block = min(n_lon, 64)
    lon_piece = 16
    basis_copy.wait()

    def convolve(block):
        for piece in range(lon_block // lon_piece):
            offset = piece * lon_piece
            first = offset if isinstance(block, int) else pl.multiple_of(block * lon_block, lon_block) + offset
            if isinstance(block, int):
                window = padded[:, first: first + lon_piece + 2 * PAD]
            else:
                window = padded[:, pl.ds(first, lon_piece + 2 * PAD)]
            shifted = [
                window[lat_step, PAD + lon_step - 2: PAD + lon_step - 2 + lon_piece]
                for lat_step in range(3)
                for lon_step in range(5)
            ]
            for b in range(basis_count):
                total = None
                for tap in range(15):
                    term = (mask_ref[0, b, tap].astype(F32) * weight_ref[0, b, tap]) * shifted[tap]
                    total = term if total is None else total + term
                taps[pl.ds(offset, lon_piece), pl.ds(b * channels, channels)] = total.astype(BF16)
        mixed = jnp.dot(
            taps[...], basis[...].reshape(basis_count * channels, channels), preferred_element_type=F32
        )
        start = block * lon_block if isinstance(block, int) else pl.multiple_of(block * lon_block, lon_block)
        grid[pl.ds(start, lon_block)] = mixed.astype(BF16)

    repeat(n_lon // lon_block, convolve)

    slabs = block_rows // width

    def transform(block):
        if not single_dft:
            dft_block(block * block_rows)
        rows = jnp.dot(table[...], grid[...], preferred_element_type=F32).astype(BF16)
        sent[pl.ds(block * slabs, slabs)] = rows.reshape(slabs, width, channels)

    repeat(2 * n_orders // block_rows, transform)

    def ord_copy(step):
        peer = lax.rem(ord_id + step, n_ord_dev)
        return pltpu.make_async_remote_copy(
            src_ref=sent.at[pl.ds(peer * groups, groups)], dst_ref=held.at[:, row_id],
            send_sem=ord_send.at[step], recv_sem=ord_recv.at[step],
            device_id=(lat_id, peer), device_id_type=MESH,
        )

    def ord_arrival(step):
        source = lat_id * n_ord_dev + lax.rem(ord_id + n_ord_dev - step, n_ord_dev)
        return pltpu.make_async_remote_copy(
            src_ref=sent.at[pl.ds(0, groups)], dst_ref=held.at[:, source],
            send_sem=ord_send.at[step], recv_sem=ord_recv.at[step],
            device_id=(lat_id, ord_id), device_id_type=MESH,
        )

    for step in range(1, n_ord_dev):
        ord_copy(step).start()
    held[:, row_id] = sent[pl.ds(ord_id * groups, groups)]
    for step in range(1, n_ord_dev):
        ord_arrival(step).wait_recv()

    def lat_copy(step):
        band = pl.ds(lat_id * n_ord_dev, n_ord_dev)
        return pltpu.make_async_remote_copy(
            src_ref=held.at[:, band], dst_ref=held.at[:, band],
            send_sem=lat_send.at[step], recv_sem=lat_recv.at[step],
            device_id=(lax.rem(lat_id + step, n_lat_dev), ord_id), device_id_type=MESH,
        )

    def lat_arrival(step):
        source = lax.rem(lat_id + n_lat_dev - step, n_lat_dev)
        band = pl.ds(source * n_ord_dev, n_ord_dev)
        return pltpu.make_async_remote_copy(
            src_ref=held.at[:, band], dst_ref=held.at[:, band],
            send_sem=lat_send.at[step], recv_sem=lat_recv.at[step],
            device_id=(lat_id, ord_id), device_id_type=MESH,
        )

    for step in range(1, n_lat_dev):
        lat_copy(step).start()
    pl.when(has_next)(to_next.wait_send)
    pl.when(has_prev)(to_prev.wait_send)
    for step in range(1, n_ord_dev):
        ord_copy(step).wait_send()
    gain_copy.wait()
    spectral_copy.wait()
    for step in range(1, n_lat_dev):
        lat_arrival(step).wait_recv()

    def latitude(group, part):
        rows = held[group, pl.ds(part * lat_rows, lat_rows)].reshape(lat_rows * width, channels)
        return jnp.dot(lat_mat[...], rows, preferred_element_type=F32)

    def finish(group):
        if single_lat:
            total = latitude(group, 0)
        else:
            def add(part, so_far):
                lat_block(group, part)
                return so_far + latitude(group, part)

            total = lax.fori_loop(
                0, n_lat // lat_rows, add, jnp.zeros((2 * out_rows, channels), F32)
            )
        gains = jnp.broadcast_to(gain[...][:, None, :], (waves, width, channels)).reshape(out_rows, channels)
        straight = (total[:out_rows] * gains).astype(BF16)
        turned = (total[out_rows:] * gains).astype(BF16)
        result = jnp.dot(straight, spectral[0], preferred_element_type=F32) + jnp.dot(
            turned, spectral[1], preferred_element_type=F32
        )
        out_ref[group] = result.astype(BF16)

    repeat(groups, finish)
    for step in range(1, n_lat_dev):
        lat_copy(step).wait_send()


def per_device(field, tap_mask, tap_weight, basis_mix, order_slots, degree_gain, spectral_mix):
    rows_here, n_lon, channels = field.shape
    assert rows_here == 1
    basis_count = basis_mix.shape[0]
    n_lat = degree_gain.shape[0]
    n_orders = order_slots.shape[0]
    n_lat_dev = lax.axis_size("lat")
    n_ord_dev = lax.axis_size("ord")
    slots_here = n_orders // n_ord_dev
    waves = n_lat // n_lat_dev
    per_slab = min(SLAB // 2, slots_here)
    width = 2 * per_slab
    groups = slots_here // per_slab
    lat_rows = min(n_lat, 256 // width)
    block_rows = min(2 * n_orders, 64)
    lon_block = min(n_lon, 64)
    out_rows = waves * width
    dims = (n_lat_dev, n_ord_dev, n_lat, n_lon, n_orders, channels, basis_count)
    smem = pl.BlockSpec(memory_space=pltpu.SMEM)
    vmem = pl.BlockSpec(memory_space=pltpu.VMEM)
    anywhere = pl.BlockSpec(memory_space=pl.ANY)
    result = pl.pallas_call(
        functools.partial(kernel, dims),
        out_shape=jax.ShapeDtypeStruct((groups, out_rows, channels), BF16),
        in_specs=[smem, smem, vmem, anywhere, anywhere, anywhere, anywhere],
        out_specs=vmem,
        scratch_shapes=[
            pltpu.VMEM((3, n_lon, channels), BF16),
            pltpu.VMEM((3, n_lon + 2 * PAD, channels), F32),
            pltpu.VMEM((lon_block, basis_count * channels), BF16),
            pltpu.VMEM((basis_count, channels, channels), BF16),
            pltpu.VMEM((waves, channels), F32),
            pltpu.VMEM((2, channels, channels), BF16),
            pltpu.VMEM((n_lon, channels), BF16),
            pltpu.VMEM((block_rows, n_lon), BF16),
            pltpu.VMEM((n_ord_dev * groups, width, channels), BF16),
            pltpu.VMEM((groups, n_lat, width, channels), BF16),
            pltpu.VMEM((2 * out_rows, lat_rows * width), BF16),
            pltpu.SemaphoreType.DMA((4,)),
            pltpu.SemaphoreType.DMA((2,)),
            pltpu.SemaphoreType.DMA((2,)),
            pltpu.SemaphoreType.DMA((n_ord_dev,)),
            pltpu.SemaphoreType.DMA((n_ord_dev,)),
            pltpu.SemaphoreType.DMA((n_lat_dev,)),
            pltpu.SemaphoreType.DMA((n_lat_dev,)),
        ],
        compiler_params=pltpu.CompilerParams(
            collective_id=0, has_side_effects=True, vmem_limit_bytes=40 * 1024 * 1024
        ),
    )(tap_mask, tap_weight, order_slots.reshape(1, n_orders), field, basis_mix, degree_gain, spectral_mix)
    result = result.reshape(groups, waves, per_slab, 2, channels)
    return jnp.swapaxes(result, 0, 1).reshape(waves, slots_here, 2, channels)


def solution(mesh):
    in_specs = (
        P(("lat", "ord"), None, None),
        P(("lat", "ord"), None, None),
        P(("lat", "ord"), None, None),
        P(),
        P(),
        P(),
        P(),
    )
    out_specs = P("lat", "ord", None, None)
    return jax.shard_map(
        per_device, mesh=mesh, in_specs=in_specs, out_specs=out_specs, check_vma=False
    )
```

```python
import functools
import math

import jax
import jax.numpy as jnp
from jax import lax
from jax.experimental import pallas as pl
from jax.experimental.pallas import tpu as pltpu
from jax.sharding import PartitionSpec as P

MESH = pl.DeviceIdType.MESH
F32 = jnp.float32
BF16 = jnp.bfloat16
PAD = 8
SLAB = 8


def log2(n):
    assert n & (n - 1) == 0
    return n.bit_length() - 1


def cosine(phase_int, period):
    q = phase_int & (period - 1)
    r = jnp.minimum(q, period - q)
    x = (period // 4 - r).astype(F32) * (2.0 * math.pi / period)
    x2 = x * x
    total = jnp.full_like(x, -1.0 / math.factorial(11))
    for power, sign in ((9, 1.0), (7, -1.0), (5, 1.0), (3, -1.0), (1, 1.0)):
        total = total * x2 + sign / math.factorial(power)
    return total * x


def iota(shape, dim):
    return lax.broadcasted_iota(jnp.int32, shape, dim)


def repeat(count, body):
    if count == 1:
        body(0)
    else:
        pl.loop(0, count)(body)


def kernel(
    dims,
    mask_hbm, weight_hbm, slots_hbm, field_hbm, basis_hbm, gain_hbm, spectral_hbm,
    out_ref,
    mask_ref, weight_ref, slots_ref, rows_in, padded, taps, basis, gain, spectral, grid, table, sent, held, lat_mat,
    local_sem, halo_send, halo_recv, ord_send, ord_recv, lat_send, lat_recv,
):
    n_lat_dev, n_ord_dev, n_lat, n_lon, n_orders, channels, basis_count = dims
    lat_id = lax.axis_index("lat")
    ord_id = lax.axis_index("ord")
    row_id = lat_id * n_ord_dev + ord_id
    slots_here = n_orders // n_ord_dev
    waves = n_lat // n_lat_dev
    per_slab = min(SLAB // 2, slots_here)
    width = 2 * per_slab
    groups = slots_here // per_slab
    has_prev = row_id > 0
    has_next = row_id < n_lat - 1
    prev_dev = ((row_id - 1) // n_ord_dev, (row_id - 1) % n_ord_dev)
    next_dev = ((row_id + 1) // n_ord_dev, (row_id + 1) % n_ord_dev)
    far_prev = jnp.logical_and(ord_id == 0, has_prev)
    far_next = jnp.logical_and(ord_id == n_ord_dev - 1, has_next)

    barrier = pltpu.get_barrier_semaphore()

    @pl.when(far_prev)
    def _():
        pl.semaphore_signal(barrier, inc=1, device_id=prev_dev, device_id_type=MESH)

    @pl.when(far_next)
    def _():
        pl.semaphore_signal(barrier, inc=1, device_id=next_dev, device_id_type=MESH)

    for step in range(1, n_ord_dev):
        pl.semaphore_signal(
            barrier, inc=1, device_id=(lat_id, lax.rem(ord_id + step, n_ord_dev)), device_id_type=MESH
        )
    for step in range(1, n_lat_dev):
        pl.semaphore_signal(
            barrier, inc=1, device_id=(lax.rem(lat_id + step, n_lat_dev), ord_id), device_id_type=MESH
        )

    own_copy = pltpu.make_async_copy(field_hbm, rows_in.at[pl.ds(1, 1)], local_sem.at[0])
    basis_copy = pltpu.make_async_copy(basis_hbm, basis, local_sem.at[1])
    gain_copy = pltpu.make_async_copy(
        gain_hbm.at[pl.ds(pl.multiple_of(lat_id * waves, waves), waves)], gain, local_sem.at[2]
    )
    spectral_copy = pltpu.make_async_copy(spectral_hbm, spectral, local_sem.at[3])
    mask_copy = pltpu.make_async_copy(mask_hbm, mask_ref, local_sem.at[4])
    weight_copy = pltpu.make_async_copy(weight_hbm, weight_ref, local_sem.at[5])
    slots_copy = pltpu.make_async_copy(slots_hbm, slots_ref, local_sem.at[6])
    slots_copy.start()
    mask_copy.start()
    weight_copy.start()
    own_copy.start()
    basis_copy.start()
    gain_copy.start()
    spectral_copy.start()

    @pl.when(jnp.logical_not(has_prev))
    def _():
        rows_in[0] = jnp.zeros(rows_in.shape[1:], BF16)

    @pl.when(jnp.logical_not(has_next))
    def _():
        rows_in[2] = jnp.zeros(rows_in.shape[1:], BF16)

    slots_copy.wait()
    orders = slots_ref[...]

    def pick(slot_of_row):
        found = iota((slot_of_row.shape[0], n_orders), 1) == slot_of_row
        return jnp.sum(jnp.where(found, orders.astype(F32), 0.0), axis=1, keepdims=True).astype(jnp.int32)

    block_rows = table.shape[0]

    def dft_block(start):
        row = iota((block_rows, 1), 0) + start
        order = pick(row >> 1)
        phase = order * iota((block_rows, n_lon), 1) + (n_lon // 4) * (row & 1)
        table[...] = (cosine(phase, n_lon) * (1.0 / math.sqrt(n_lon))).astype(BF16)

    lat_rows = min(n_lat, 256 // width)
    out_rows = waves * width

    def lat_block(group, part):
        row = iota((out_rows, 1), 0)
        col = iota((1, lat_rows * width), 1)
        wave = (row >> log2(width)) + lat_id * waves
        slot = (row & (width - 1)) >> 1
        order = pick(slot + ord_id * slots_here + group * per_slab)
        lat = (col >> log2(width)) + part * lat_rows
        phase = wave * (2 * lat + 1) + jnp.where((order & 1) == 0, 0, 3 * n_lat)
        value = cosine(phase, 4 * n_lat) * math.sqrt(2.0 / n_lat)
        apart = (row & (width - 1)) ^ (col & (width - 1))
        straight = jnp.where(apart == 0, value, 0.0)
        turned = jnp.where(apart == 1, jnp.where((row & 1) == 0, -value, value), 0.0)
        lat_mat[:out_rows] = straight.astype(BF16)
        lat_mat[out_rows:] = turned.astype(BF16)

    single_dft = block_rows == 2 * n_orders
    single_lat = groups == 1 and lat_rows == n_lat
    if single_dft:
        dft_block(0)

    others = (n_ord_dev - 1) + (n_lat_dev - 1)
    pl.semaphore_wait(barrier, others + far_prev.astype(jnp.int32) + far_next.astype(jnp.int32))

    to_next = pltpu.make_async_remote_copy(
        src_ref=field_hbm, dst_ref=rows_in.at[pl.ds(0, 1)], send_sem=halo_send.at[0],
        recv_sem=halo_recv.at[0], device_id=next_dev, device_id_type=MESH,
    )
    to_prev = pltpu.make_async_remote_copy(
        src_ref=field_hbm, dst_ref=rows_in.at[pl.ds(2, 1)], send_sem=halo_send.at[1],
        recv_sem=halo_recv.at[1], device_id=prev_dev, device_id_type=MESH,
    )
    pl.when(has_next)(to_next.start)
    pl.when(has_prev)(to_prev.start)
    if single_lat:
        lat_block(0, 0)

    def spread(which):
        row = rows_in[which].astype(F32)
        padded[which, pl.ds(PAD, n_lon)] = row
        padded[which, pl.ds(0, PAD)] = row[n_lon - PAD:]
        padded[which, pl.ds(PAD + n_lon, PAD)] = row[:PAD]

    own_copy.wait()
    spread(1)
    pl.when(has_prev)(to_next.wait_recv)
    spread(0)
    pl.when(has_next)(to_prev.wait_recv)
    spread(2)

    lon_block = min(n_lon, 64)
    lon_piece = 16
    basis_copy.wait()
    mask_copy.wait()
    weight_copy.wait()

    def convolve(block):
        for piece in range(lon_block // lon_piece):
            offset = piece * lon_piece
            first = offset if isinstance(block, int) else pl.multiple_of(block * lon_block, lon_block) + offset
            if isinstance(block, int):
                window = padded[:, first: first + lon_piece + 2 * PAD]
            else:
                window = padded[:, pl.ds(first, lon_piece + 2 * PAD)]
            shifted = [
                window[lat_step, PAD + lon_step - 2: PAD + lon_step - 2 + lon_piece]
                for lat_step in range(3)
                for lon_step in range(5)
            ]
            for b in range(basis_count):
                total = None
                for tap in range(15):
                    term = (mask_ref[0, b, tap].astype(F32) * weight_ref[0, b, tap]) * shifted[tap]
                    total = term if total is None else total + term
                taps[pl.ds(offset, lon_piece), pl.ds(b * channels, channels)] = total.astype(BF16)
        mixed = jnp.dot(
            taps[...], basis[...].reshape(basis_count * channels, channels), preferred_element_type=F32
        )
        start = block * lon_block if isinstance(block, int) else pl.multiple_of(block * lon_block, lon_block)
        grid[pl.ds(start, lon_block)] = mixed.astype(BF16)

    repeat(n_lon // lon_block, convolve)

    slabs = block_rows // width

    def transform(block):
        if not single_dft:
            dft_block(block * block_rows)
        rows = jnp.dot(table[...], grid[...], preferred_element_type=F32).astype(BF16)
        sent[pl.ds(block * slabs, slabs)] = rows.reshape(slabs, width, channels)

    repeat(2 * n_orders // block_rows, transform)

    def ord_copy(step):
        peer = lax.rem(ord_id + step, n_ord_dev)
        return pltpu.make_async_remote_copy(
            src_ref=sent.at[pl.ds(peer * groups, groups)], dst_ref=held.at[:, row_id],
            send_sem=ord_send.at[step], recv_sem=ord_recv.at[step],
            device_id=(lat_id, peer), device_id_type=MESH,
        )

    def ord_arrival(step):
        source = lat_id * n_ord_dev + lax.rem(ord_id + n_ord_dev - step, n_ord_dev)
        return pltpu.make_async_remote_copy(
            src_ref=sent.at[pl.ds(0, groups)], dst_ref=held.at[:, source],
            send_sem=ord_send.at[step], recv_sem=ord_recv.at[step],
            device_id=(lat_id, ord_id), device_id_type=MESH,
        )

    for step in range(1, n_ord_dev):
        ord_copy(step).start()
    held[:, row_id] = sent[pl.ds(ord_id * groups, groups)]
    for step in range(1, n_ord_dev):
        ord_arrival(step).wait_recv()

    def lat_copy(step):
        band = pl.ds(lat_id * n_ord_dev, n_ord_dev)
        return pltpu.make_async_remote_copy(
            src_ref=held.at[:, band], dst_ref=held.at[:, band],
            send_sem=lat_send.at[step], recv_sem=lat_recv.at[step],
            device_id=(lax.rem(lat_id + step, n_lat_dev), ord_id), device_id_type=MESH,
        )

    def lat_arrival(step):
        source = lax.rem(lat_id + n_lat_dev - step, n_lat_dev)
        band = pl.ds(source * n_ord_dev, n_ord_dev)
        return pltpu.make_async_remote_copy(
            src_ref=held.at[:, band], dst_ref=held.at[:, band],
            send_sem=lat_send.at[step], recv_sem=lat_recv.at[step],
            device_id=(lat_id, ord_id), device_id_type=MESH,
        )

    for step in range(1, n_lat_dev):
        lat_copy(step).start()
    pl.when(has_next)(to_next.wait_send)
    pl.when(has_prev)(to_prev.wait_send)
    for step in range(1, n_ord_dev):
        ord_copy(step).wait_send()
    gain_copy.wait()
    spectral_copy.wait()
    for step in range(1, n_lat_dev):
        lat_arrival(step).wait_recv()

    def latitude(group, part):
        rows = held[group, pl.ds(part * lat_rows, lat_rows)].reshape(lat_rows * width, channels)
        return jnp.dot(lat_mat[...], rows, preferred_element_type=F32)

    def finish(group):
        if single_lat:
            total = latitude(group, 0)
        else:
            def add(part, so_far):
                lat_block(group, part)
                return so_far + latitude(group, part)

            total = lax.fori_loop(
                0, n_lat // lat_rows, add, jnp.zeros((2 * out_rows, channels), F32)
            )
        gains = jnp.broadcast_to(gain[...][:, None, :], (waves, width, channels)).reshape(out_rows, channels)
        straight = (total[:out_rows] * gains).astype(BF16)
        turned = (total[out_rows:] * gains).astype(BF16)
        result = jnp.dot(straight, spectral[0], preferred_element_type=F32) + jnp.dot(
            turned, spectral[1], preferred_element_type=F32
        )
        out_ref[group] = result.astype(BF16)

    repeat(groups, finish)
    for step in range(1, n_lat_dev):
        lat_copy(step).wait_send()


def per_device(field, tap_mask, tap_weight, basis_mix, order_slots, degree_gain, spectral_mix):
    rows_here, n_lon, channels = field.shape
    assert rows_here == 1
    basis_count = basis_mix.shape[0]
    n_lat = degree_gain.shape[0]
    n_orders = order_slots.shape[0]
    n_lat_dev = lax.axis_size("lat")
    n_ord_dev = lax.axis_size("ord")
    slots_here = n_orders // n_ord_dev
    waves = n_lat // n_lat_dev
    per_slab = min(SLAB // 2, slots_here)
    width = 2 * per_slab
    groups = slots_here // per_slab
    lat_rows = min(n_lat, 256 // width)
    block_rows = min(2 * n_orders, 64)
    lon_block = min(n_lon, 64)
    out_rows = waves * width
    dims = (n_lat_dev, n_ord_dev, n_lat, n_lon, n_orders, channels, basis_count)
    vmem = pl.BlockSpec(memory_space=pltpu.VMEM)
    hbm = pl.BlockSpec(memory_space=pltpu.HBM)
    result = pl.pallas_call(
        functools.partial(kernel, dims),
        out_shape=jax.ShapeDtypeStruct((groups, out_rows, channels), BF16),
        in_specs=[hbm] * 7,
        out_specs=vmem,
        scratch_shapes=[
            pltpu.SMEM(tap_mask.shape, jnp.int32),
            pltpu.SMEM(tap_weight.shape, F32),
            pltpu.VMEM((1, n_orders), jnp.int32),
            pltpu.VMEM((3, n_lon, channels), BF16),
            pltpu.VMEM((3, n_lon + 2 * PAD, channels), F32),
            pltpu.VMEM((lon_block, basis_count * channels), BF16),
            pltpu.VMEM((basis_count, channels, channels), BF16),
            pltpu.VMEM((waves, channels), F32),
            pltpu.VMEM((2, channels, channels), BF16),
            pltpu.VMEM((n_lon, channels), BF16),
            pltpu.VMEM((block_rows, n_lon), BF16),
            pltpu.VMEM((n_ord_dev * groups, width, channels), BF16),
            pltpu.VMEM((groups, n_lat, width, channels), BF16),
            pltpu.VMEM((2 * out_rows, lat_rows * width), BF16),
            pltpu.SemaphoreType.DMA((7,)),
            pltpu.SemaphoreType.DMA((2,)),
            pltpu.SemaphoreType.DMA((2,)),
            pltpu.SemaphoreType.DMA((n_ord_dev,)),
            pltpu.SemaphoreType.DMA((n_ord_dev,)),
            pltpu.SemaphoreType.DMA((n_lat_dev,)),
            pltpu.SemaphoreType.DMA((n_lat_dev,)),
        ],
        compiler_params=pltpu.CompilerParams(
            collective_id=0, has_side_effects=True, vmem_limit_bytes=63 * 1024 * 1024
        ),
    )(tap_mask, tap_weight, order_slots.reshape(1, n_orders), field, basis_mix, degree_gain, spectral_mix)
    result = result.reshape(groups, waves, per_slab, 2, channels)
    return jnp.swapaxes(result, 0, 1).reshape(waves, slots_here, 2, channels)


def solution(mesh):
    in_specs = (
        P(("lat", "ord"), None, None),
        P(("lat", "ord"), None, None),
        P(("lat", "ord"), None, None),
        P(),
        P(),
        P(),
        P(),
    )
    out_specs = P("lat", "ord", None, None)
    return jax.shard_map(
        per_device, mesh=mesh, in_specs=in_specs, out_specs=out_specs, check_vma=False
    )
```

```python
import functools
import math

import jax
import jax.numpy as jnp
from jax import lax
from jax.experimental import pallas as pl
from jax.experimental.pallas import tpu as pltpu
from jax.sharding import PartitionSpec as P

MESH = pl.DeviceIdType.MESH
F32 = jnp.float32
BF16 = jnp.bfloat16
PAD = 8
SLAB = 8


def log2(n):
    assert n & (n - 1) == 0
    return n.bit_length() - 1


def cosine(phase_int, period):
    q = phase_int & (period - 1)
    r = jnp.minimum(q, period - q)
    x = (period // 4 - r).astype(F32) * (2.0 * math.pi / period)
    x2 = x * x
    total = jnp.full_like(x, -1.0 / math.factorial(11))
    for power, sign in ((9, 1.0), (7, -1.0), (5, 1.0), (3, -1.0), (1, 1.0)):
        total = total * x2 + sign / math.factorial(power)
    return total * x


def iota(shape, dim):
    return lax.broadcasted_iota(jnp.int32, shape, dim)


def repeat(count, body):
    if count == 1:
        body(0)
    else:
        pl.loop(0, count)(body)


def kernel(
    dims,
    mask_hbm, weight_hbm, slots_hbm, field_hbm, basis_hbm, gain_hbm, spectral_hbm,
    out_ref,
    mask_ref, weight_ref, slots_ref, rows_in, padded, taps, basis, gain, spectral, grid, table, sent, held, lat_mat,
    local_sem, halo_send, halo_recv, all_send, all_recv, band_sem,
):
    n_lat_dev, n_ord_dev, n_lat, n_lon, n_orders, channels, basis_count = dims
    lat_id = lax.axis_index("lat")
    ord_id = lax.axis_index("ord")
    row_id = lat_id * n_ord_dev + ord_id
    slots_here = n_orders // n_ord_dev
    waves = n_lat // n_lat_dev
    per_slab = min(SLAB // 2, slots_here)
    width = 2 * per_slab
    groups = slots_here // per_slab
    has_prev = row_id > 0
    has_next = row_id < n_lat - 1
    ord_mask = n_ord_dev - 1
    at_first = (ord_id == 0).astype(jnp.int32)
    at_last = (ord_id == ord_mask).astype(jnp.int32)
    prev_dev = (lat_id - at_first, (ord_id + ord_mask) & ord_mask)
    next_dev = (lat_id + at_last, (ord_id + 1) & ord_mask)
    count = n_lat_dev * n_ord_dev
    ord_bits = log2(n_ord_dev)
    assert log2(count) == log2(n_lat_dev) + ord_bits
    far_prev = jnp.logical_and(ord_id == 0, has_prev)
    far_next = jnp.logical_and(ord_id == n_ord_dev - 1, has_next)

    barrier = pltpu.get_barrier_semaphore()

    @pl.when(far_prev)
    def _():
        pl.semaphore_signal(barrier, inc=1, device_id=prev_dev, device_id_type=MESH)

    @pl.when(far_next)
    def _():
        pl.semaphore_signal(barrier, inc=1, device_id=next_dev, device_id_type=MESH)

    for step in range(n_ord_dev - 1, 0, -1):
        pl.semaphore_signal(barrier, inc=1, device_id=(lat_id, ord_id ^ step), device_id_type=MESH)
    for step in range(1, n_lat_dev):
        pl.semaphore_signal(barrier, inc=1, device_id=(lat_id ^ step, ord_id), device_id_type=MESH)

    own_copy = pltpu.make_async_copy(field_hbm, rows_in.at[pl.ds(1, 1)], local_sem.at[0])
    basis_copy = pltpu.make_async_copy(basis_hbm, basis, local_sem.at[1])
    gain_copy = pltpu.make_async_copy(
        gain_hbm.at[pl.ds(pl.multiple_of(lat_id * waves, waves), waves)], gain, local_sem.at[2]
    )
    spectral_copy = pltpu.make_async_copy(spectral_hbm, spectral, local_sem.at[3])
    mask_copy = pltpu.make_async_copy(mask_hbm, mask_ref, local_sem.at[4])
    weight_copy = pltpu.make_async_copy(weight_hbm, weight_ref, local_sem.at[5])
    slots_copy = pltpu.make_async_copy(slots_hbm, slots_ref, local_sem.at[6])
    slots_copy.start()
    mask_copy.start()
    weight_copy.start()
    own_copy.start()
    basis_copy.start()
    gain_copy.start()
    spectral_copy.start()

    @pl.when(jnp.logical_not(has_prev))
    def _():
        rows_in[0] = jnp.zeros(rows_in.shape[1:], BF16)

    @pl.when(jnp.logical_not(has_next))
    def _():
        rows_in[2] = jnp.zeros(rows_in.shape[1:], BF16)

    slots_copy.wait()
    orders = slots_ref[...]

    def pick(slot_of_row):
        found = iota((slot_of_row.shape[0], n_orders), 1) == slot_of_row
        return jnp.sum(jnp.where(found, orders.astype(F32), 0.0), axis=1, keepdims=True).astype(jnp.int32)

    block_rows = table.shape[0]

    def dft_block(start):
        row = iota((block_rows, 1), 0) + start
        order = pick(row >> 1)
        phase = order * iota((block_rows, n_lon), 1) + (n_lon // 4) * (row & 1)
        table[...] = (cosine(phase, n_lon) * (1.0 / math.sqrt(n_lon))).astype(BF16)

    lat_rows = min(n_lat, 256 // width)
    out_rows = waves * width

    def lat_block(group, part):
        row = iota((out_rows, 1), 0)
        col = iota((1, lat_rows * width), 1)
        wave = (row >> log2(width)) + lat_id * waves
        slot = (row & (width - 1)) >> 1
        order = pick(slot + ord_id * slots_here + group * per_slab)
        lat = (col >> log2(width)) + part * lat_rows
        phase = wave * (2 * lat + 1) + jnp.where((order & 1) == 0, 0, 3 * n_lat)
        value = cosine(phase, 4 * n_lat) * math.sqrt(2.0 / n_lat)
        apart = (row & (width - 1)) ^ (col & (width - 1))
        straight = jnp.where(apart == 0, value, 0.0)
        turned = jnp.where(apart == 1, jnp.where((row & 1) == 0, -value, value), 0.0)
        lat_mat[:out_rows] = straight.astype(BF16)
        lat_mat[out_rows:] = turned.astype(BF16)

    single_dft = block_rows == 2 * n_orders
    single_lat = groups == 1 and lat_rows == n_lat
    if single_dft:
        dft_block(0)

    pl.semaphore_wait(
        barrier, (n_ord_dev - 1) + (n_lat_dev - 1) + far_prev.astype(jnp.int32) + far_next.astype(jnp.int32)
    )

    to_next = pltpu.make_async_remote_copy(
        src_ref=field_hbm, dst_ref=rows_in.at[pl.ds(0, 1)], send_sem=halo_send.at[0],
        recv_sem=halo_recv.at[0], device_id=next_dev, device_id_type=MESH,
    )
    to_prev = pltpu.make_async_remote_copy(
        src_ref=field_hbm, dst_ref=rows_in.at[pl.ds(2, 1)], send_sem=halo_send.at[1],
        recv_sem=halo_recv.at[1], device_id=prev_dev, device_id_type=MESH,
    )
    pl.when(has_next)(to_next.start)
    pl.when(has_prev)(to_prev.start)
    for step in range(1, n_lat_dev):
        pl.semaphore_signal(band_sem, inc=1, device_id=(lat_id ^ step, ord_id), device_id_type=MESH)
    if single_lat:
        lat_block(0, 0)

    def spread(which):
        row = rows_in[which].astype(F32)
        padded[which, pl.ds(PAD, n_lon)] = row
        padded[which, pl.ds(0, PAD)] = row[n_lon - PAD:]
        padded[which, pl.ds(PAD + n_lon, PAD)] = row[:PAD]

    own_copy.wait()
    spread(1)
    pl.when(has_prev)(to_next.wait_recv)
    spread(0)
    pl.when(has_next)(to_prev.wait_recv)
    spread(2)

    lon_block = min(n_lon, 64)
    lon_piece = 16
    basis_copy.wait()
    mask_copy.wait()
    weight_copy.wait()

    def convolve(block):
        for piece in range(lon_block // lon_piece):
            offset = piece * lon_piece
            first = offset if isinstance(block, int) else pl.multiple_of(block * lon_block, lon_block) + offset
            if isinstance(block, int):
                window = padded[:, first: first + lon_piece + 2 * PAD]
            else:
                window = padded[:, pl.ds(first, lon_piece + 2 * PAD)]
            shifted = [
                window[lat_step, PAD + lon_step - 2: PAD + lon_step - 2 + lon_piece]
                for lat_step in range(3)
                for lon_step in range(5)
            ]
            for b in range(basis_count):
                total = None
                for tap in range(15):
                    term = (mask_ref[0, b, tap].astype(F32) * weight_ref[0, b, tap]) * shifted[tap]
                    total = term if total is None else total + term
                taps[pl.ds(offset, lon_piece), pl.ds(b * channels, channels)] = total.astype(BF16)
        mixed = jnp.dot(
            taps[...], basis[...].reshape(basis_count * channels, channels), preferred_element_type=F32
        )
        start = block * lon_block if isinstance(block, int) else pl.multiple_of(block * lon_block, lon_block)
        grid[pl.ds(start, lon_block)] = mixed.astype(BF16)

    repeat(n_lon // lon_block, convolve)

    slabs = block_rows // width

    def transform(block):
        if not single_dft:
            dft_block(block * block_rows)
        rows = jnp.dot(table[...], grid[...], preferred_element_type=F32).astype(BF16)
        sent[pl.ds(block * slabs, slabs)] = rows.reshape(slabs, width, channels)

    repeat(2 * n_orders // block_rows, transform)

    def send(step):
        lat_step, ord_step = step >> ord_bits, step & ord_mask
        target = (lat_id ^ lat_step, ord_id ^ ord_step)
        pltpu.make_async_remote_copy(
            src_ref=sent.at[pl.ds(target[1] * groups, groups)], dst_ref=held.at[:, row_id],
            send_sem=all_send.at[0], recv_sem=all_recv.at[0],
            device_id=target, device_id_type=MESH,
        ).start()

    pl.semaphore_wait(band_sem, n_lat_dev - 1)
    if count <= 64:
        for step in sorted(range(1, count), key=lambda step: (-(step & ord_mask), -step)):
            send(step)
    else:
        pl.loop(1, count)(send)
    held[:, row_id] = sent[pl.ds(ord_id * groups, groups)]
    pl.when(has_next)(to_next.wait_send)
    pl.when(has_prev)(to_prev.wait_send)
    gain_copy.wait()
    spectral_copy.wait()
    arrivals = pltpu.make_async_remote_copy(
        src_ref=held.at[:, pl.ds(0, count - 1)], dst_ref=held.at[:, pl.ds(0, count - 1)],
        send_sem=all_send.at[0], recv_sem=all_recv.at[0],
        device_id=(lat_id, ord_id ^ 1), device_id_type=MESH,
    )
    arrivals.wait_recv()

    def latitude(group, part):
        rows = held[group, pl.ds(part * lat_rows, lat_rows)].reshape(lat_rows * width, channels)
        return jnp.dot(lat_mat[...], rows, preferred_element_type=F32)

    def finish(group):
        if single_lat:
            total = latitude(group, 0)
        else:
            def add(part, so_far):
                lat_block(group, part)
                return so_far + latitude(group, part)

            total = lax.fori_loop(
                0, n_lat // lat_rows, add, jnp.zeros((2 * out_rows, channels), F32)
            )
        gains = jnp.broadcast_to(gain[...][:, None, :], (waves, width, channels)).reshape(out_rows, channels)
        straight = (total[:out_rows] * gains).astype(BF16)
        turned = (total[out_rows:] * gains).astype(BF16)
        result = jnp.dot(straight, spectral[0], preferred_element_type=F32) + jnp.dot(
            turned, spectral[1], preferred_element_type=F32
        )
        out_ref[group] = result.astype(BF16)

    repeat(groups, finish)
    arrivals.wait_send()


def per_device(field, tap_mask, tap_weight, basis_mix, order_slots, degree_gain, spectral_mix):
    rows_here, n_lon, channels = field.shape
    assert rows_here == 1
    basis_count = basis_mix.shape[0]
    n_lat = degree_gain.shape[0]
    n_orders = order_slots.shape[0]
    n_lat_dev = lax.axis_size("lat")
    n_ord_dev = lax.axis_size("ord")
    slots_here = n_orders // n_ord_dev
    waves = n_lat // n_lat_dev
    per_slab = min(SLAB // 2, slots_here)
    width = 2 * per_slab
    groups = slots_here // per_slab
    lat_rows = min(n_lat, 256 // width)
    block_rows = min(2 * n_orders, 64)
    lon_block = min(n_lon, 64)
    out_rows = waves * width
    dims = (n_lat_dev, n_ord_dev, n_lat, n_lon, n_orders, channels, basis_count)
    vmem = pl.BlockSpec(memory_space=pltpu.VMEM)
    hbm = pl.BlockSpec(memory_space=pltpu.HBM)
    result = pl.pallas_call(
        functools.partial(kernel, dims),
        out_shape=jax.ShapeDtypeStruct((groups, out_rows, channels), BF16),
        in_specs=[hbm] * 7,
        out_specs=vmem,
        scratch_shapes=[
            pltpu.SMEM(tap_mask.shape, jnp.int32),
            pltpu.SMEM(tap_weight.shape, F32),
            pltpu.VMEM((1, n_orders), jnp.int32),
            pltpu.VMEM((3, n_lon, channels), BF16),
            pltpu.VMEM((3, n_lon + 2 * PAD, channels), F32),
            pltpu.VMEM((lon_block, basis_count * channels), BF16),
            pltpu.VMEM((basis_count, channels, channels), BF16),
            pltpu.VMEM((waves, channels), F32),
            pltpu.VMEM((2, channels, channels), BF16),
            pltpu.VMEM((n_lon, channels), BF16),
            pltpu.VMEM((block_rows, n_lon), BF16),
            pltpu.VMEM((n_ord_dev * groups, width, channels), BF16),
            pltpu.VMEM((groups, n_lat, width, channels), BF16),
            pltpu.VMEM((2 * out_rows, lat_rows * width), BF16),
            pltpu.SemaphoreType.DMA((7,)),
            pltpu.SemaphoreType.DMA((2,)),
            pltpu.SemaphoreType.DMA((2,)),
            pltpu.SemaphoreType.DMA((1,)),
            pltpu.SemaphoreType.DMA((1,)),
            pltpu.SemaphoreType.REGULAR,
        ],
        compiler_params=pltpu.CompilerParams(
            collective_id=0, has_side_effects=True, vmem_limit_bytes=63 * 1024 * 1024
        ),
    )(tap_mask, tap_weight, order_slots.reshape(1, n_orders), field, basis_mix, degree_gain, spectral_mix)
    result = result.reshape(groups, waves, per_slab, 2, channels)
    return jnp.swapaxes(result, 0, 1).reshape(waves, slots_here, 2, channels)


def solution(mesh):
    in_specs = (
        P(("lat", "ord"), None, None),
        P(("lat", "ord"), None, None),
        P(("lat", "ord"), None, None),
        P(),
        P(),
        P(),
        P(),
    )
    out_specs = P("lat", "ord", None, None)
    return jax.shard_map(
        per_device, mesh=mesh, in_specs=in_specs, out_specs=out_specs, check_vma=False
    )
```

```python
import functools
import math

import jax
import jax.numpy as jnp
from jax import lax
from jax.experimental import pallas as pl
from jax.experimental.pallas import tpu as pltpu
from jax.sharding import PartitionSpec as P

MESH = pl.DeviceIdType.MESH
F32 = jnp.float32
BF16 = jnp.bfloat16
PAD = 8
SLAB = 8


def log2(n):
    assert n & (n - 1) == 0
    return n.bit_length() - 1


def cosine(phase_int, period):
    q = phase_int & (period - 1)
    r = jnp.minimum(q, period - q)
    x = (period // 4 - r).astype(F32) * (2.0 * math.pi / period)
    x2 = x * x
    total = jnp.full_like(x, -1.0 / math.factorial(11))
    for power, sign in ((9, 1.0), (7, -1.0), (5, 1.0), (3, -1.0), (1, 1.0)):
        total = total * x2 + sign / math.factorial(power)
    return total * x


def iota(shape, dim):
    return lax.broadcasted_iota(jnp.int32, shape, dim)


def repeat(count, body):
    if count == 1:
        body(0)
    else:
        pl.loop(0, count)(body)


def kernel(
    dims,
    mask_hbm, weight_hbm, slots_hbm, field_hbm, basis_hbm, gain_hbm, spectral_hbm,
    out_ref,
    mask_ref, weight_ref, slots_ref, rows_in, padded, partial, taps, basis, gain, spectral, grid, table, sent, held, lat_mat,
    local_sem, halo_send, halo_recv, all_send, all_recv, band_sem,
):
    n_lat_dev, n_ord_dev, n_lat, n_lon, n_orders, channels, basis_count = dims
    lat_id = lax.axis_index("lat")
    ord_id = lax.axis_index("ord")
    row_id = lat_id * n_ord_dev + ord_id
    slots_here = n_orders // n_ord_dev
    waves = n_lat // n_lat_dev
    per_slab = min(SLAB // 2, slots_here)
    width = 2 * per_slab
    groups = slots_here // per_slab
    has_prev = row_id > 0
    has_next = row_id < n_lat - 1
    ord_mask = n_ord_dev - 1
    at_first = (ord_id == 0).astype(jnp.int32)
    at_last = (ord_id == ord_mask).astype(jnp.int32)
    prev_dev = (lat_id - at_first, (ord_id + ord_mask) & ord_mask)
    next_dev = (lat_id + at_last, (ord_id + 1) & ord_mask)
    count = n_lat_dev * n_ord_dev
    ord_bits = log2(n_ord_dev)
    assert log2(count) == log2(n_lat_dev) + ord_bits
    far_prev = jnp.logical_and(ord_id == 0, has_prev)
    far_next = jnp.logical_and(ord_id == n_ord_dev - 1, has_next)

    barrier = pltpu.get_barrier_semaphore()

    @pl.when(far_prev)
    def _():
        pl.semaphore_signal(barrier, inc=1, device_id=prev_dev, device_id_type=MESH)

    @pl.when(far_next)
    def _():
        pl.semaphore_signal(barrier, inc=1, device_id=next_dev, device_id_type=MESH)

    for step in range(n_ord_dev - 1, 0, -1):
        pl.semaphore_signal(barrier, inc=1, device_id=(lat_id, ord_id ^ step), device_id_type=MESH)
    for step in range(1, n_lat_dev):
        pl.semaphore_signal(barrier, inc=1, device_id=(lat_id ^ step, ord_id), device_id_type=MESH)

    own_copy = pltpu.make_async_copy(field_hbm, rows_in.at[pl.ds(1, 1)], local_sem.at[0])
    basis_copy = pltpu.make_async_copy(basis_hbm, basis, local_sem.at[1])
    gain_copy = pltpu.make_async_copy(
        gain_hbm.at[pl.ds(pl.multiple_of(lat_id * waves, waves), waves)], gain, local_sem.at[2]
    )
    spectral_copy = pltpu.make_async_copy(spectral_hbm, spectral, local_sem.at[3])
    mask_copy = pltpu.make_async_copy(mask_hbm, mask_ref, local_sem.at[4])
    weight_copy = pltpu.make_async_copy(weight_hbm, weight_ref, local_sem.at[5])
    slots_copy = pltpu.make_async_copy(slots_hbm, slots_ref, local_sem.at[6])
    slots_copy.start()
    mask_copy.start()
    weight_copy.start()
    own_copy.start()
    basis_copy.start()
    gain_copy.start()
    spectral_copy.start()

    @pl.when(jnp.logical_not(has_prev))
    def _():
        rows_in[0] = jnp.zeros(rows_in.shape[1:], BF16)

    @pl.when(jnp.logical_not(has_next))
    def _():
        rows_in[2] = jnp.zeros(rows_in.shape[1:], BF16)

    slots_copy.wait()
    orders = slots_ref[...]

    def pick(slot_of_row):
        found = iota((slot_of_row.shape[0], n_orders), 1) == slot_of_row
        return jnp.sum(jnp.where(found, orders.astype(F32), 0.0), axis=1, keepdims=True).astype(jnp.int32)

    block_rows = table.shape[0]

    def dft_block(start):
        row = iota((block_rows, 1), 0) + start
        order = pick(row >> 1)
        phase = order * iota((block_rows, n_lon), 1) + (n_lon // 4) * (row & 1)
        table[...] = (cosine(phase, n_lon) * (1.0 / math.sqrt(n_lon))).astype(BF16)

    lat_rows = min(n_lat, 256 // width)
    out_rows = waves * width

    def lat_block(group, part):
        row = iota((out_rows, 1), 0)
        col = iota((1, lat_rows * width), 1)
        wave = (row >> log2(width)) + lat_id * waves
        slot = (row & (width - 1)) >> 1
        order = pick(slot + ord_id * slots_here + group * per_slab)
        lat = (col >> log2(width)) + part * lat_rows
        phase = wave * (2 * lat + 1) + jnp.where((order & 1) == 0, 0, 3 * n_lat)
        value = cosine(phase, 4 * n_lat) * math.sqrt(2.0 / n_lat)
        apart = (row & (width - 1)) ^ (col & (width - 1))
        straight = jnp.where(apart == 0, value, 0.0)
        turned = jnp.where(apart == 1, jnp.where((row & 1) == 0, -value, value), 0.0)
        lat_mat[:out_rows] = straight.astype(BF16)
        lat_mat[out_rows:] = turned.astype(BF16)

    single_dft = block_rows == 2 * n_orders
    single_lat = groups == 1 and lat_rows == n_lat
    if single_dft:
        dft_block(0)

    own_copy.wait()
    pl.semaphore_wait(
        barrier, (n_ord_dev - 1) + (n_lat_dev - 1) + far_prev.astype(jnp.int32) + far_next.astype(jnp.int32)
    )

    to_next = pltpu.make_async_remote_copy(
        src_ref=rows_in.at[pl.ds(1, 1)], dst_ref=rows_in.at[pl.ds(0, 1)], send_sem=halo_send.at[0],
        recv_sem=halo_recv.at[0], device_id=next_dev, device_id_type=MESH,
    )
    to_prev = pltpu.make_async_remote_copy(
        src_ref=rows_in.at[pl.ds(1, 1)], dst_ref=rows_in.at[pl.ds(2, 1)], send_sem=halo_send.at[1],
        recv_sem=halo_recv.at[1], device_id=prev_dev, device_id_type=MESH,
    )
    pl.when(has_next)(to_next.start)
    pl.when(has_prev)(to_prev.start)
    for step in range(1, n_lat_dev):
        pl.semaphore_signal(band_sem, inc=1, device_id=(lat_id ^ step, ord_id), device_id_type=MESH)
    if single_lat:
        lat_block(0, 0)

    def spread(which):
        row = rows_in[which].astype(F32)
        padded[which, pl.ds(PAD, n_lon)] = row
        padded[which, pl.ds(0, PAD)] = row[n_lon - PAD:]
        padded[which, pl.ds(PAD + n_lon, PAD)] = row[:PAD]

    lon_block = min(n_lon, 64)
    lon_piece = 16

    def tap_terms(lat_steps, block, piece, b, total):
        first = block * lon_block + piece * lon_piece
        for lat_step in lat_steps:
            if isinstance(block, int):
                window = padded[lat_step, first: first + lon_piece + 2 * PAD]
            else:
                window = padded[lat_step, pl.ds(pl.multiple_of(first, lon_piece), lon_piece + 2 * PAD)]
            for lon_step in range(5):
                tap = 5 * lat_step + lon_step
                shifted = window[PAD + lon_step - 2: PAD + lon_step - 2 + lon_piece]
                term = (mask_ref[0, b, tap].astype(F32) * weight_ref[0, b, tap]) * shifted
                total = term if total is None else total + term
        return total

    def place(block, piece):
        first = block * lon_block + piece * lon_piece
        return pl.ds(first if isinstance(block, int) else pl.multiple_of(first, lon_piece), lon_piece)

    def middle(block):
        for piece in range(lon_block // lon_piece):
            for b in range(basis_count):
                partial[b, place(block, piece)] = tap_terms((1,), block, piece, b, None)

    def convolve(block):
        for piece in range(lon_block // lon_piece):
            for b in range(basis_count):
                total = tap_terms((0, 2), block, piece, b, partial[b, place(block, piece)])
                taps[pl.ds(piece * lon_piece, lon_piece), pl.ds(b * channels, channels)] = total.astype(BF16)
        mixed = jnp.dot(
            taps[...], basis[...].reshape(basis_count * channels, channels), preferred_element_type=F32
        )
        start = block * lon_block if isinstance(block, int) else pl.multiple_of(block * lon_block, lon_block)
        grid[pl.ds(start, lon_block)] = mixed.astype(BF16)

    spread(1)
    mask_copy.wait()
    weight_copy.wait()
    repeat(n_lon // lon_block, middle)
    basis_copy.wait()
    pl.when(has_prev)(to_next.wait_recv)
    spread(0)
    pl.when(has_next)(to_prev.wait_recv)
    spread(2)
    repeat(n_lon // lon_block, convolve)

    slabs = block_rows // width

    def transform(block):
        if not single_dft:
            dft_block(block * block_rows)
        rows = jnp.dot(table[...], grid[...], preferred_element_type=F32).astype(BF16)
        sent[pl.ds(block * slabs, slabs)] = rows.reshape(slabs, width, channels)

    repeat(2 * n_orders // block_rows, transform)

    def send(step):
        lat_step, ord_step = step >> ord_bits, step & ord_mask
        target = (lat_id ^ lat_step, ord_id ^ ord_step)
        pltpu.make_async_remote_copy(
            src_ref=sent.at[pl.ds(target[1] * groups, groups)], dst_ref=held.at[:, row_id],
            send_sem=all_send.at[0], recv_sem=all_recv.at[0],
            device_id=target, device_id_type=MESH,
        ).start()

    pl.semaphore_wait(band_sem, n_lat_dev - 1)
    if count <= 64:
        for step in sorted(range(1, count), key=lambda step: (-(step & ord_mask), -step)):
            send(step)
    else:
        pl.loop(1, count)(send)
    held[:, row_id] = sent[pl.ds(ord_id * groups, groups)]
    pl.when(has_next)(to_next.wait_send)
    pl.when(has_prev)(to_prev.wait_send)
    gain_copy.wait()
    spectral_copy.wait()
    arrivals = pltpu.make_async_remote_copy(
        src_ref=held.at[:, pl.ds(0, count - 1)], dst_ref=held.at[:, pl.ds(0, count - 1)],
        send_sem=all_send.at[0], recv_sem=all_recv.at[0],
        device_id=(lat_id, ord_id ^ 1), device_id_type=MESH,
    )
    arrivals.wait_recv()

    def latitude(group, part):
        rows = held[group, pl.ds(part * lat_rows, lat_rows)].reshape(lat_rows * width, channels)
        return jnp.dot(lat_mat[...], rows, preferred_element_type=F32)

    def finish(group):
        if single_lat:
            total = latitude(group, 0)
        else:
            def add(part, so_far):
                lat_block(group, part)
                return so_far + latitude(group, part)

            total = lax.fori_loop(
                0, n_lat // lat_rows, add, jnp.zeros((2 * out_rows, channels), F32)
            )
        gains = jnp.broadcast_to(gain[...][:, None, :], (waves, width, channels)).reshape(out_rows, channels)
        straight = (total[:out_rows] * gains).astype(BF16)
        turned = (total[out_rows:] * gains).astype(BF16)
        result = jnp.dot(straight, spectral[0], preferred_element_type=F32) + jnp.dot(
            turned, spectral[1], preferred_element_type=F32
        )
        out_ref[group] = result.astype(BF16)

    repeat(groups, finish)
    arrivals.wait_send()


def per_device(field, tap_mask, tap_weight, basis_mix, order_slots, degree_gain, spectral_mix):
    rows_here, n_lon, channels = field.shape
    assert rows_here == 1
    basis_count = basis_mix.shape[0]
    n_lat = degree_gain.shape[0]
    n_orders = order_slots.shape[0]
    n_lat_dev = lax.axis_size("lat")
    n_ord_dev = lax.axis_size("ord")
    slots_here = n_orders // n_ord_dev
    waves = n_lat // n_lat_dev
    per_slab = min(SLAB // 2, slots_here)
    width = 2 * per_slab
    groups = slots_here // per_slab
    lat_rows = min(n_lat, 256 // width)
    block_rows = min(2 * n_orders, 64)
    lon_block = min(n_lon, 64)
    out_rows = waves * width
    dims = (n_lat_dev, n_ord_dev, n_lat, n_lon, n_orders, channels, basis_count)
    vmem = pl.BlockSpec(memory_space=pltpu.VMEM)
    hbm = pl.BlockSpec(memory_space=pltpu.HBM)
    result = pl.pallas_call(
        functools.partial(kernel, dims),
        out_shape=pltpu.VMEM((groups, out_rows, channels), BF16),
        in_specs=[hbm] * 7,
        out_specs=vmem,
        scratch_shapes=[
            pltpu.SMEM(tap_mask.shape, jnp.int32),
            pltpu.SMEM(tap_weight.shape, F32),
            pltpu.VMEM((1, n_orders), jnp.int32),
            pltpu.VMEM((3, n_lon, channels), BF16),
            pltpu.VMEM((3, n_lon + 2 * PAD, channels), F32),
            pltpu.VMEM((basis_count, n_lon, channels), F32),
            pltpu.VMEM((lon_block, basis_count * channels), BF16),
            pltpu.VMEM((basis_count, channels, channels), BF16),
            pltpu.VMEM((waves, channels), F32),
            pltpu.VMEM((2, channels, channels), BF16),
            pltpu.VMEM((n_lon, channels), BF16),
            pltpu.VMEM((block_rows, n_lon), BF16),
            pltpu.VMEM((n_ord_dev * groups, width, channels), BF16),
            pltpu.VMEM((groups, n_lat, width, channels), BF16),
            pltpu.VMEM((2 * out_rows, lat_rows * width), BF16),
            pltpu.SemaphoreType.DMA((7,)),
            pltpu.SemaphoreType.DMA((2,)),
            pltpu.SemaphoreType.DMA((2,)),
            pltpu.SemaphoreType.DMA((1,)),
            pltpu.SemaphoreType.DMA((1,)),
            pltpu.SemaphoreType.REGULAR,
        ],
        compiler_params=pltpu.CompilerParams(
            collective_id=0, has_side_effects=True, vmem_limit_bytes=63 * 1024 * 1024
        ),
    )(*[pltpu.with_memory_space_constraint(x, pltpu.HBM) for x in (tap_mask, tap_weight, order_slots.reshape(1, n_orders), field, basis_mix, degree_gain, spectral_mix)])
    result = result.reshape(groups, waves, per_slab, 2, channels)
    return jnp.swapaxes(result, 0, 1).reshape(waves, slots_here, 2, channels)


def solution(mesh):
    in_specs = (
        P(("lat", "ord"), None, None),
        P(("lat", "ord"), None, None),
        P(("lat", "ord"), None, None),
        P(),
        P(),
        P(),
        P(),
    )
    out_specs = P("lat", "ord", None, None)
    return jax.shard_map(
        per_device, mesh=mesh, in_specs=in_specs, out_specs=out_specs, check_vma=False
    )
```
